128 devices in a mesh: gx: 8 (over y, core), yz: 16 (over z, x).
Axes of the slice: x: 4, y: 4, z: 4, core: 2. Of those that a mesh axis runs over, the one named last changes fastest.
Arguments:
- tokens: bfloat16 [768, 12288], P(None, ('gx', 'yz')), may hold values from -6 to 6
- gate_weight: bfloat16 [12288, 36864], P('gx', 'yz'), may hold values from -0.078125 to 0.078125
- up_weight: bfloat16 [12288, 36864], P('gx', 'yz'), may hold values from -0.078125 to 0.078125
- down_weight: bfloat16 [36864, 12288], P('yz', 'gx'), may hold values from -0.046875 to 0.046875
Outputs:
- mixed: bfloat16 [768, 12288], P(None, ('gx', 'yz'))
The draws below stay inside these ranges and needn't reach their ends.
All inputs are finite; a program needn't handle non-finite values.
Results may differ from the reference program's by a relative error of at most 0.03.
Values may be sent and summed in bfloat16 or wider, within the bound.
A program may use at most 128 MiB of HBM per device.

```python
import jax
import jax.numpy as jnp
from jax import lax

D = 12288
FF = 36864
ROWS = 768
N_GX = 8


def raised(drawn, stream_key, source, target, parts, factor):
    def block_of(dim):
        return (jnp.arange(drawn.shape[dim]) // (drawn.shape[dim] // parts)).reshape((-1,) + (1,) * (drawn.ndim - 1 - dim))

    one_side = jax.random.permutation(stream_key, parts)[block_of(target)]
    second = (block_of(target) + parts // 2) % parts
    return jnp.where((block_of(source) == one_side) | (block_of(source) == second), factor * drawn, drawn)


def shard_levels(key, shape, split, low, top_value):
    factor_of, own = 1.0, jax.random.fold_in(key, 6)
    for axis_at, blocks in split:
        steps = jnp.exp(jax.random.uniform(jax.random.fold_in(own, axis_at), (blocks,), jnp.float32, low / len(split), top_value / len(split)))
        factor_of = factor_of * jnp.repeat(steps, shape[axis_at] // blocks).reshape([-1 if axis == axis_at else 1 for axis in range(len(shape))])
    return factor_of


def bell_draw(rng, extent, scale, most, pieces=(), dtype=jnp.bfloat16):
    level = shard_levels(rng, extent, pieces, -0.22, 0.18) if pieces else 1.0
    result = jax.random.normal(rng, extent, jnp.float32) * scale * level
    return jnp.minimum(jnp.maximum(result, -most), most).astype(dtype)


def bell_draw_with(key, dims, scale, limit, shards, heavy, dtype=jnp.bfloat16):
    result = scale * jax.random.normal(key, dims, jnp.float32)
    if shards:
        result = result * shard_levels(key, dims, shards, -0.22, 0.18)
    return jnp.clip(raised(result, jax.random.fold_in(key, 3), *heavy), -limit, limit).astype(dtype)


def setup_inputs(seed: int = 0) -> dict:
    key_of = jax.random.split(jax.random.key(seed), 5)
    tokens = bell_draw(key_of[0], (ROWS, D), 1.0, 6.0, ((1, 128),))
    gate_weight = bell_draw_with(key_of[1], (D, FF), D ** -0.5, 0.078125, ((0, 8), (1, 16)), (0, 1, 16, 2.0))
    up_weight = bell_draw_with(key_of[2], (D, FF), D ** -0.5, 0.078125, ((0, 8), (1, 16)), (0, 1, 16, 2.0))
    down_weight = bell_draw_with(key_of[3], (FF, D), FF ** -0.5, 0.046875, ((0, 16), (1, 8)), (0, 1, 16, 2.0))
    return {"tokens": tokens, "gate_weight": gate_weight, "up_weight": up_weight, "down_weight": down_weight}


def reference(tokens, gate_weight, up_weight, down_weight):
    width = D // N_GX
    gate = jnp.zeros((ROWS, FF), jnp.float32)
    up = jnp.zeros((ROWS, FF), jnp.float32)
    for block in range(N_GX):
        part_tokens = tokens[:, block * width:(block + 1) * width]
        gate_part = jnp.dot(part_tokens, gate_weight[block * width:(block + 1) * width], preferred_element_type=jnp.float32).astype(jnp.bfloat16)
        up_part = jnp.dot(part_tokens, up_weight[block * width:(block + 1) * width], preferred_element_type=jnp.float32).astype(jnp.bfloat16)
        gate_part, up_part = lax.optimization_barrier((gate_part, up_part))
        gate = gate + gate_part.astype(jnp.float32)
        up = up + up_part.astype(jnp.float32)
    hidden = (jax.nn.silu(gate) * up).astype(jnp.bfloat16)
    return jnp.dot(hidden, down_weight, preferred_element_type=jnp.float32).astype(jnp.bfloat16)
```

```python
import functools

import jax
import jax.numpy as jnp
from jax import lax
from jax.experimental import pallas as pl
from jax.experimental.pallas import tpu as pltpu
from jax.sharding import PartitionSpec as P

BF = jnp.bfloat16
F32 = jnp.float32
MESH = pl.DeviceIdType.MESH

ROWS = 768
R = 192
NI = ROWS // R
NJ = 3
S = NI * NJ
Q = R // 4
H = R // 2
K = 1536
FF = 2304
FH = FF // 2
FB = FH // NJ
ZB = 384
XB = 96


def kernel(tok_hbm, wg_hbm, wu_hbm, wd_hbm, out,
           wgu, wd, tok, tokx, sibs, sibr, par, own, yr, hid, terms, zr, xs, xr,
           w_sem, wd_sem, tl_sem, tx_s, tx_r, tz_s, tz_r,
           d_s, d_r, y_s, y_r, h_s, h_r, f_s, f_r, z_s, z_r, x_s, x_r):
    g = lax.axis_index("gx")
    s_ = lax.axis_index("yz")
    y, c = g // 2, g % 2
    z, x = s_ // 4, s_ % 4

    def m4(v):
        return lax.rem(v, 4)

    def at_y(v):
        return (m4(v) * 2 + c, s_)

    def at_z(v):
        return (g, m4(v) * 4 + x)

    def at_x(v):
        return (g, z * 4 + m4(v))

    sib_dev = (y * 2 + 1 - c, s_)
    yp, ym = at_y(y + 1), at_y(y + 3)
    zp, zm = at_z(z + 1), at_z(z + 3)
    xp, xm, xo = at_x(x + 1), at_x(x + 3), at_x(x + 2)

    def rc(src, dst, ss, rs, dev):
        return pltpu.make_async_remote_copy(
            src_ref=src, dst_ref=dst, send_sem=ss, recv_sem=rs,
            device_id=dev, device_id_type=MESH)

    def rows(q, n):
        return pl.ds(pl.multiple_of(q * n, 16), n)

    def lanes(b, n):
        return pl.ds(pl.multiple_of(b * n, 128), n)

    def w_copies(b):
        cols = lanes(b, FB)
        return (pltpu.make_async_copy(wg_hbm.at[:, cols], wgu.at[b, :, pl.ds(0, FB)], w_sem.at[b, 0]),
                pltpu.make_async_copy(wu_hbm.at[:, cols], wgu.at[b, :, pl.ds(FB, FB)], w_sem.at[b, 1]))

    def b_sib(j):
        return (1 - c) * NJ + j

    def b_own(j):
        return c * NJ + j

    tok_local = pltpu.make_async_copy(tok_hbm, tokx.at[x], tl_sem)
    tok_local.start()

    barrier = pltpu.get_barrier_semaphore()
    partners = (sib_dev, yp, ym, zp, zm, xp, xm, xo)
    for dev in partners:
        pl.semaphore_signal(barrier, inc=1, device_id=dev, device_id_type=MESH)
    for j in range(NJ):
        for b in (b_sib(j), b_own(j)):
            for cp in w_copies(b):
                cp.start()
    wd_copy = pltpu.make_async_copy(wd_hbm, wd, wd_sem)
    wd_copy.start()
    pl.semaphore_wait(barrier, len(partners))

    def tx_copy(i, d, dev):
        rr = rows(i, R)
        return rc(tok_hbm.at[rr], tokx.at[x, rr], tx_s.at[i, d], tx_r.at[i, d], dev)

    for i in range(NI):
        for d, dev in enumerate((xp, xm, xo)):
            tx_copy(i, d, dev).start()

    def tz_copy(i, d):
        blk = tok.at[i, :, lanes(z, ZB)]
        return rc(blk, blk, tz_s.at[i, d], tz_r.at[i, d], zp if d == 0 else zm)

    def tz_recv(i, d):
        blk = tok.at[i, :, lanes(m4(z + 3) if d == 0 else m4(z + 1), ZB)]
        return rc(blk, blk, tz_s.at[i, d], tz_r.at[i, d], zp)

    def tf_copy(i, d):
        blk = tok.at[i, pl.ds(d * H, H), lanes(m4(z + 3) if d == 0 else m4(z + 1), ZB)]
        return rc(blk, blk, tz_s.at[i, 2 + d], tz_r.at[i, 2 + d], zp if d == 0 else zm)

    def tf_recv(i, d):
        blk = tok.at[i, pl.ds(d * H, H), lanes(m4(z + 2), ZB)]
        return rc(blk, blk, tz_s.at[i, 2 + d], tz_r.at[i, 2 + d], zp)

    def tok_spread(i):
        rr = rows(i, R)
        for d, dev in enumerate((xp, xm, xo)):
            tx_copy(i, d, dev).wait()
        tok[i, :, lanes(z, ZB)] = jnp.concatenate([tokx[k, rr, :] for k in range(4)], axis=1)
        for d in range(2):
            tz_copy(i, d).start()

    def tok_forward(i):
        for d in range(2):
            tz_recv(i, d).wait_recv()
            tf_copy(i, d).start()

    def tok_ready(i):
        for d in range(2):
            tf_recv(i, d).wait_recv()
            tz_copy(i, d).wait_send()
            tf_copy(i, d).wait_send()

    tok_local.wait()
    tok_spread(0)
    tok_forward(0)
    tok_spread(1)

    def d_copy(s):
        return rc(sibs.at[s], sibr.at[s], d_s.at[s], d_r.at[s], sib_dev)

    def stage_sib(s):
        i, j = s // NJ, s % NJ

        @pl.when(j == 0)
        def _():
            tok_ready(i)

        @pl.when(i == 0)
        def _():
            for cp in w_copies(b_sib(j)):
                cp.wait()

        sibs[s] = jnp.dot(tok[i], wgu[b_sib(j)], preferred_element_type=F32).astype(BF)
        d_copy(s).start()

    def stage_own(s):
        i, j = s // NJ, s % NJ

        @pl.when(i == 0)
        def _():
            for cp in w_copies(b_own(j)):
                cp.wait()

        own[...] = jnp.dot(tok[i], wgu[b_own(j)], preferred_element_type=F32)

    G, U = pl.ds(0, FB), pl.ds(FB, FB)

    def y_copy(s, n):
        if n == 0:
            src, dev = par.at[s, rows(m4(y + 2), Q), G], yp
        elif n == 1:
            src, dev = par.at[s, rows(m4(y + 2), Q), U], ym
        elif n == 2:
            src, dev = par.at[s, rows(m4(y + 1), Q), U], yp
        elif n == 3:
            src, dev = par.at[s, rows(m4(y + 3), Q), G], ym
        elif n == 4:
            src, dev = par.at[s, rows(m4(y + 1), Q), G], yp
        else:
            src, dev = par.at[s, rows(m4(y + 3), Q), U], ym
        return rc(src, yr.at[s, n], y_s.at[s, n], y_r.at[s, n], dev)

    def stage_merge(s):
        d_copy(s).wait()
        par[s] = (own[...] + sibr[s].astype(F32)).astype(BF)
        for n in range(4):
            y_copy(s, n).start()

    def stage_c(s):
        y_copy(s, 0).wait()
        rr = rows(m4(y + 1), Q)
        par[s, rr, G] = (par[s, rr, G].astype(F32) + yr[s, 0].astype(F32)).astype(BF)
        y_copy(s, 4).start()
        y_copy(s, 1).wait()
        rr = rows(m4(y + 3), Q)
        par[s, rr, U] = (par[s, rr, U].astype(F32) + yr[s, 1].astype(F32)).astype(BF)
        y_copy(s, 5).start()

    def h_block(s, yy):
        i, j = s // NJ, s % NJ
        return hid.at[i, rows(m4(yy), Q), lanes(b_own(j), FB)]

    def h_copy(s, d):
        blk = h_block(s, y)
        return rc(blk, blk, h_s.at[s, d], h_r.at[s, d], yp if d == 0 else ym)

    def h_recv(s, d):
        blk = h_block(s, y + 3 if d == 0 else y + 1)
        return rc(blk, blk, h_s.at[s, d], h_r.at[s, d], yp)

    def hf_copy(s, d):
        blk = h_block(s, y + 3 if d == 0 else y + 1)
        return rc(blk, blk, h_s.at[s, 2], h_r.at[s, 2], yp if d == 0 else ym)

    def hf_recv(s):
        blk = h_block(s, y + 2)
        return rc(blk, blk, h_s.at[s, 2], h_r.at[s, 2], yp)

    def stage_d(s):
        i, j = s // NJ, s % NJ
        for n in range(2, 6):
            y_copy(s, n).wait()
        rr = rows(y, Q)
        gate = par[s, rr, G].astype(F32) + (yr[s, 3].astype(F32) + yr[s, 4].astype(F32))
        up = par[s, rr, U].astype(F32) + (yr[s, 2].astype(F32) + yr[s, 5].astype(F32))
        hid[i, rr, lanes(b_own(j), FB)] = (gate / (1.0 + jnp.exp(-gate)) * up).astype(BF)
        for d in range(2):
            h_copy(s, d).start()

    def stage_e(s):
        for d in range(2):
            h_copy(s, d).wait_send()
            h_recv(s, d).wait_recv()

        @pl.when(s % 2 == 0)
        def _():
            hf_copy(s, 0).start()

        @pl.when(s % 2 == 1)
        def _():
            hf_copy(s, 1).start()

    def f_copy(s, half):
        i, j = s // NJ, s % NJ
        blk = hid.at[i, :, lanes(half * NJ + j, FB)]
        return rc(blk, blk, f_s.at[s], f_r.at[s], sib_dev)

    def stage_f(s):
        hf_recv(s).wait_recv()
        hf_copy(s, 0).wait_send()
        f_copy(s, c).start()

    def zb(k):
        return lanes(m4(z + k), ZB)

    A, B = pl.ds(0, H), pl.ds(H, H)

    def z_copy(i, n):
        half, k, dev = ((A, 2, zp), (B, 2, zm), (B, 1, zp), (A, 3, zm), (A, 1, zp), (B, 3, zm))[n]
        return rc(terms.at[i, half, zb(k)], zr.at[i, n], z_s.at[i, n], z_r.at[i, n], dev)

    def stage_g(i):
        @pl.when(i == 0)
        def _():
            wd_copy.wait()

        for j in range(NJ):
            f_copy(i * NJ + j, c).wait_send()
            f_copy(i * NJ + j, 1 - c).wait_recv()
        first = m4(z + 2) // 2
        for n in range(2):
            cols = lanes(first if n == 0 else 1 - first, 2 * ZB)
            terms[i, :, cols] = jnp.dot(hid[i], wd[:, cols], preferred_element_type=F32).astype(BF)
            if n == 0:
                z_copy(i, 0).start()
                z_copy(i, 1).start()
        z_copy(i, 2).start()
        z_copy(i, 3).start()

    def stage_z(i):
        z_copy(i, 0).wait()
        terms[i, A, zb(1)] = (terms[i, A, zb(1)].astype(F32) + zr[i, 0].astype(F32)).astype(BF)
        z_copy(i, 4).start()
        z_copy(i, 1).wait()
        terms[i, B, zb(3)] = (terms[i, B, zb(3)].astype(F32) + zr[i, 1].astype(F32)).astype(BF)
        z_copy(i, 5).start()

    def x_copy(i, d):
        k, dev = ((1, xp), (3, xm), (2, xo))[d]
        return rc(xs.at[i, m4(x + k)], xr.at[i, d], x_s.at[i, d], x_r.at[i, d], dev)

    def stage_x(i):
        for n in range(2, 6):
            z_copy(i, n).wait()
        for half, n1, n2 in ((A, 3, 4), (B, 2, 5)):
            v = terms[i, half, zb(0)].astype(F32) + (zr[i, n1].astype(F32) + zr[i, n2].astype(F32))
            for k in range(4):
                xs[i, k, half, :] = v[:, k * XB:(k + 1) * XB].astype(BF)
        for d in range(3):
            x_copy(i, d).start()

    def stage_out(i):
        for d in range(3):
            x_copy(i, d).wait()
        v = xs[i, x].astype(F32)
        for d in range(3):
            v = v + xr[i, d].astype(F32)
        out[rows(i, R), :] = v.astype(BF)

    def step(u, _):
        t = u - 1

        @pl.when((t >= 0) & (t < S))
        def _():
            stage_own(t)

        @pl.when(t + 1 < S)
        def _():
            stage_sib(t + 1)

        @pl.when((t >= 0) & (t < S))
        def _():
            stage_merge(t)

        def lag(n, f):
            s = t - n

            @pl.when((s >= 0) & (s < S))
            def _():
                f(s)

        def lag_i(n, f):
            s = t - n

            @pl.when((s >= 0) & (s < S) & (lax.rem(s + S, NJ) == NJ - 1))
            def _():
                f(s // NJ)

        lag(1, stage_c)
        lag(2, stage_d)
        lag(3, stage_e)
        lag(4, stage_f)

        i, j = t // NJ, t % NJ

        @pl.when((t >= 0) & (j == 0) & (i + 1 < NI))
        def _():
            tok_forward(i + 1)

            @pl.when(i + 2 < NI)
            def _():
                tok_spread(i + 2)

        lag_i(5, stage_g)
        lag_i(6, stage_z)
        lag_i(7, stage_x)
        lag_i(8, stage_out)
        return 0

    lax.fori_loop(0, S + 9, step, 0)


def body(tokens, gate_weight, up_weight, down_weight):
    V = pltpu.VMEM
    D = pltpu.SemaphoreType.DMA
    return pl.pallas_call(
        kernel,
        out_shape=jax.ShapeDtypeStruct((ROWS, XB), BF),
        in_specs=[pl.BlockSpec(memory_space=pl.ANY)] * 4,
        out_specs=pl.BlockSpec(memory_space=V),
        scratch_shapes=[
            V((2 * NJ, K, 2 * FB), BF),
            V((FF, K), BF),
            V((NI, R, K), BF),
            V((4, ROWS, XB), BF),
            V((S, R, 2 * FB), BF),
            V((S, R, 2 * FB), BF),
            V((S, R, 2 * FB), BF),
            V((R, 2 * FB), F32),
            V((S, 6, Q, FB), BF),
            V((NI, R, FF), BF),
            V((NI, R, K), BF),
            V((NI, 6, H, ZB), BF),
            V((NI, 4, R, XB), BF),
            V((NI, 3, R, XB), BF),
            D((2 * NJ, 2)), D(()), D(()),
            D((NI, 3)), D((NI, 3)), D((NI, 4)), D((NI, 4)),
            D((S,)), D((S,)), D((S, 6)), D((S, 6)), D((S, 3)), D((S, 3)), D((S,)), D((S,)),
            D((NI, 6)), D((NI, 6)), D((NI, 3)), D((NI, 3)),
        ],
        compiler_params=pltpu.CompilerParams(
            collective_id=0, has_side_effects=True, vmem_limit_bytes=60 * 2**20),
    )(tokens, gate_weight, up_weight, down_weight)


def solution(mesh):
    placed = (P(None, ("gx", "yz")), P("gx", "yz"), P("gx", "yz"), P("yz", "gx"))
    return jax.shard_map(
        body, mesh=mesh, in_specs=placed, out_specs=P(None, ("gx", "yz")), check_vma=False
    )
```

```python
import jax
import jax.numpy as jnp
from jax import lax
from jax.experimental import pallas as pl
from jax.experimental.pallas import tpu as pltpu
from jax.sharding import PartitionSpec as P

BF = jnp.bfloat16
F32 = jnp.float32
MESH = pl.DeviceIdType.MESH

ROWS = 768
R = 128
NI = ROWS // R
NJ = 3
S = NI * NJ
Q = R // 4
K = 1536
FF = 2304
FB = FF // 2 // NJ
XB = 96
HB = XB // 2

LC, LD, LE, LF, LG, LZ, LO = 3, 5, 7, 9, 10, 12, 14
DIRECT = S - 1


def kernel(tok_hbm, wg_hbm, wu_hbm, wd_hbm, out,
           wgu, wd, tok, tokr, sibs, sibr, par, own, yr, hid, terms, r1, r2,
           w_sem, wd_sem, tl_sem, t1_s, t1_r, t2_s, t2_r,
           d_s, d_r, y_s, c_r, e_r, h_s, h_r, hf_r, f_s, f_r, z1_s, z1_r, z2_s, z2_r):
    g = lax.axis_index("gx")
    s_ = lax.axis_index("yz")
    y, c = g // 2, g % 2
    z, x = s_ // 4, s_ % 4

    def m4(v):
        return lax.rem(v, 4)

    sib_dev = (y * 2 + 1 - c, s_)
    yp, ym, yo = (m4(y + 1) * 2 + c, s_), (m4(y + 3) * 2 + c, s_), (m4(y + 2) * 2 + c, s_)

    def at_z(k):
        return (g, m4(z + k) * 4 + x)

    def at_x(k):
        return (g, z * 4 + m4(x + k))

    def rc(src, dst, ss, rs, dev):
        return pltpu.make_async_remote_copy(
            src_ref=src, dst_ref=dst, send_sem=ss, recv_sem=rs,
            device_id=dev, device_id_type=MESH)

    def arrived(ref, sem):
        rc(ref, ref, y_s, sem, sib_dev).wait_recv()

    def sent(ref, sem):
        rc(ref, ref, sem, d_r.at[0], sib_dev).wait_send()

    def rows(q, n):
        return pl.ds(pl.multiple_of(q * n, 16), n)

    def lanes(b, n):
        return pl.ds(pl.multiple_of(b * n, 128), n)

    A, B = pl.ds(0, HB), pl.ds(HB, HB)

    barrier = pltpu.get_barrier_semaphore()
    partners = [sib_dev, yp, ym, yo] + [f(k) for k in (1, 2, 3) for f in (at_z, at_x)]
    for dev in partners:
        pl.semaphore_signal(barrier, inc=1, device_id=dev, device_id_type=MESH)

    def b_sib(j):
        return (1 - c) * NJ + j

    def b_own(j):
        return c * NJ + j

    def tl_copy(i):
        return pltpu.make_async_copy(tok_hbm.at[:, pl.ds(i * R, R)], tok.at[i, z, x], tl_sem)

    for i in range(NI):
        tl_copy(i).start()

    def w_copies(b):
        cols = lanes(b, FB)
        return (pltpu.make_async_copy(wg_hbm.at[:, cols], wgu.at[b, :, pl.ds(0, FB)], w_sem.at[b]),
                pltpu.make_async_copy(wu_hbm.at[:, cols], wgu.at[b, :, pl.ds(FB, FB)], w_sem.at[b]))

    def w_arrived(b):
        pltpu.make_async_copy(wgu.at[b], wgu.at[b], w_sem.at[b]).wait()

    wd_copy = pltpu.make_async_copy(wd_hbm, wd, wd_sem)

    def weights_start():
        for j in range(NJ):
            for b in (b_sib(j), b_own(j)):
                for cp in w_copies(b):
                    cp.start()
        wd_copy.start()

    def t1_copy(i, h, k):
        cols = pl.ds(pl.multiple_of(i * R, R), R)
        half = A if h == 0 else B
        return rc(tok_hbm.at[half, cols], tok.at[i, z, x, half], t1_s, t1_r.at[i],
                  at_x(k) if h == 0 else at_z(k))

    def t2_copy(i, h, k):
        blk = tok.at[i, z, :, A] if h == 0 else tok.at[i, :, x, B]
        return rc(blk, blk, t2_s, t2_r.at[i], at_z(k) if h == 0 else at_x(k))

    BOTH = [(h, k) for k in (2, 1, 3) for h in (0, 1)]

    def tok_first(i):
        for h, k in BOTH:
            t1_copy(i, h, k).start()

    def tok_second(i):
        arrived(r2.at[i], t1_r.at[i])
        for h, k in BOTH:
            t2_copy(i, h, k).start()

    def tok_ready(i):
        arrived(r1.at[i], t2_r.at[i])
        tokr[i % 2] = tok[i].reshape(K, R).T

    def entry_barrier():
        pl.semaphore_wait(barrier, len(partners))

    def entry_own():
        pltpu.make_async_copy(tok.at[:, 0, 0], tok.at[:, 0, 0], tl_sem).wait()

    entry_barrier()
    tok_first(0)
    weights_start()
    entry_own()
    tok_second(0)
    tok_first(1)

    def d_copy(s):
        return rc(sibs.at[s], sibr.at[s], d_s, d_r.at[s], sib_dev)

    def stage_sib(s):
        i, j = s // NJ, s % NJ

        @pl.when(j == 0)
        def _():
            tok_ready(i)

        @pl.when(i == 0)
        def _():
            w_arrived(b_sib(j))

        sibs[s] = jnp.dot(tokr[i % 2], wgu[b_sib(j)], preferred_element_type=F32).astype(BF)
        d_copy(s).start()

        @pl.when((j == 0) & (i + 1 < NI))
        def _():
            tok_second(i + 1)

            @pl.when(i + 2 < NI)
            def _():
                tok_first(i + 2)

    def stage_own(s):
        i, j = s // NJ, s % NJ

        @pl.when(i == 0)
        def _():
            w_arrived(b_own(j))

        own[...] = jnp.dot(tokr[i % 2], wgu[b_own(j)], preferred_element_type=F32)

    G, U = pl.ds(0, FB), pl.ds(FB, FB)

    def y_copy(s, n):
        q, cols, dev = ((2, G, yp), (2, U, ym), (1, U, yp), (3, G, ym), (1, G, yp), (3, U, ym))[n]
        return rc(par.at[s, rows(m4(y + q), Q), cols], yr.at[s, n], y_s, (c_r if n < 2 else e_r).at[s], dev)

    def stage_merge(s):
        arrived(sibr.at[s], d_r.at[s])
        par[s] = (own[...] + sibr[s].astype(F32)).astype(BF)
        for n in range(4):
            y_copy(s, n).start()

    def stage_c(s):
        arrived(yr.at[s, pl.ds(0, 2)], c_r.at[s])
        rr = rows(m4(y + 1), Q)
        par[s, rr, G] = (par[s, rr, G].astype(F32) + yr[s, 0].astype(F32)).astype(BF)
        y_copy(s, 4).start()
        rr = rows(m4(y + 3), Q)
        par[s, rr, U] = (par[s, rr, U].astype(F32) + yr[s, 1].astype(F32)).astype(BF)
        y_copy(s, 5).start()

    def h_block(s, k):
        i, j = s // NJ, s % NJ
        return hid.at[i, rows(m4(y + k), Q), lanes(b_own(j), FB)]

    def h_copy(s, d):
        blk = h_block(s, 0)
        return rc(blk, blk, h_s, h_r.at[s], yp if d == 0 else ym)

    def hf_copy(s, d):
        blk = h_block(s, 3 if d == 0 else 1)
        return rc(blk, blk, h_s, hf_r.at[s], yp if d == 0 else ym)

    def ho_copy(s):
        blk = h_block(s, 0)
        return rc(blk, blk, h_s, hf_r.at[s], yo)

    def stage_d(s):
        i, j = s // NJ, s % NJ
        arrived(yr.at[s, pl.ds(2, 4)], e_r.at[s])
        rr = rows(y, Q)
        gate = par[s, rr, G].astype(F32) + (yr[s, 3].astype(F32) + yr[s, 4].astype(F32))
        up = par[s, rr, U].astype(F32) + (yr[s, 2].astype(F32) + yr[s, 5].astype(F32))
        hid[i, rr, lanes(b_own(j), FB)] = (gate / (1.0 + jnp.exp(-gate)) * up).astype(BF)
        @pl.when(s >= DIRECT)
        def _():
            ho_copy(s).start()

        for d in range(2):
            h_copy(s, d).start()

    def stage_e(s):
        arrived(yr.at[s, pl.ds(0, 2)], h_r.at[s])

        @pl.when((s < DIRECT) & (s % 2 == 0))
        def _():
            hf_copy(s, 0).start()

        @pl.when((s < DIRECT) & (s % 2 == 1))
        def _():
            hf_copy(s, 1).start()

    def f_copy(s, half):
        i, j = s // NJ, s % NJ
        blk = hid.at[i, :, lanes(half * NJ + j, FB)]
        return rc(blk, blk, f_s, f_r.at[i], sib_dev)

    def stage_f(s):
        arrived(yr.at[s, 0], hf_r.at[s])
        f_copy(s, c).start()

    def z1_copy(i, h, k):
        if h == 0:
            src, dev = terms.at[i, m4(z + k), :, A], at_z(k)
        else:
            src, dev = terms.at[i, :, m4(x + k), B], at_x(k)
        return rc(src, r1.at[i, h, k - 1], z1_s, z1_r.at[i], dev)

    def z2_copy(i, h, k):
        if h == 0:
            src, dev = terms.at[i, z, m4(x + k), A], at_x(k)
        else:
            src, dev = terms.at[i, m4(z + k), x, B], at_z(k)
        return rc(src, r2.at[i, h, k - 1], z2_s, z2_r.at[i], dev)

    def stage_g(i):
        @pl.when(i == 0)
        def _():
            wd_copy.wait()

        arrived(hid.at[i, :, pl.ds(0, FF // 2)], f_r.at[i])
        mine = z // 2
        for n in range(2):
            p = mine if n else 1 - mine
            res = jnp.dot(hid[i], wd[:, lanes(p, K // 2)], preferred_element_type=F32).astype(BF)
            terms[i, pl.ds(2 * p, 2)] = res.T.reshape(2, 4, XB, R)
        for h, k in BOTH:
            z1_copy(i, h, k).start()

    def stage_z(i):
        arrived(r1.at[i], z1_r.at[i])
        for h in (0, 1):
            v = r1[i, h, 0].astype(F32) + r1[i, h, 1].astype(F32) + r1[i, h, 2].astype(F32)
            if h == 0:
                terms[i, z, :, A] = (terms[i, z, :, A].astype(F32) + v).astype(BF)
            else:
                terms[i, :, x, B] = (terms[i, :, x, B].astype(F32) + v).astype(BF)
            for k in (2, 1, 3):
                z2_copy(i, h, k).start()

    def stage_out(i):
        cols = lanes(i, R)
        arrived(r2.at[i], z2_r.at[i])
        for h, half in ((0, A), (1, B)):
            v = terms[i, z, x, half].astype(F32)
            for k in (0, 1, 2):
                v = v + r2[i, h, k].astype(F32)
            out[half, cols] = v.astype(BF)

    def step(u, _):
        t = u - 1

        @pl.when((t >= 0) & (t < S))
        def _():
            stage_own(t)
            stage_merge(t)

        @pl.when(t + 1 < S)
        def _():
            stage_sib(t + 1)

        def lag(n, f):
            s = t - n

            @pl.when((s >= 0) & (s < S))
            def _():
                f(s)

        def lag_i(n, f, most):
            s = t - n

            @pl.when((s >= 0) & (s < most * NJ) & (lax.rem(s + S, NJ) == NJ - 1))
            def _():
                f(s // NJ)

        lag(LC, stage_c)
        lag(LD, stage_d)
        lag(LE, stage_e)
        lag(LF, stage_f)
        lag_i(LG, stage_g, NI - 1)
        lag_i(LZ, stage_z, NI - 2)
        lag_i(LO, stage_out, NI - 2)
        return 0

    lax.fori_loop(0, S + LF + 1, step, 0)
    stage_g(NI - 1)
    stage_z(NI - 2)
    stage_z(NI - 1)
    stage_out(NI - 2)
    stage_out(NI - 1)

    def entry_sent():
        for ref, sem in ((r2, t1_s), (r1, t2_s), (sibs, d_s), (yr, y_s), (yr.at[:, pl.ds(0, 3)], h_s),
                         (hid.at[:, :, pl.ds(0, FF // 2)], f_s), (r1, z1_s), (r2, z2_s)):
            sent(ref, sem)

    entry_sent()


def body(tokens, gate_weight, up_weight, down_weight):
    V = pltpu.VMEM
    D = pltpu.SemaphoreType.DMA
    result = pl.pallas_call(
        kernel,
        out_shape=jax.ShapeDtypeStruct((XB, ROWS), BF),
        in_specs=[pl.BlockSpec(memory_space=pl.ANY)] * 4,
        out_specs=pl.BlockSpec(memory_space=V),
        scratch_shapes=[
            V((2 * NJ, K, 2 * FB), BF),
            V((FF, K), BF),
            V((NI, 4, 4, XB, R), BF),
            V((2, R, K), BF),
            V((S, R, 2 * FB), BF),
            V((S, R, 2 * FB), BF),
            V((S, R, 2 * FB), BF),
            V((R, 2 * FB), F32),
            V((S, 6, Q, FB), BF),
            V((NI, R, FF), BF),
            V((NI, 4, 4, XB, R), BF),
            V((NI, 2, 3, 4, HB, R), BF),
            V((NI, 2, 3, HB, R), BF),
            D((2 * NJ,)), D(()), D(()),
            D(()), D((NI,)), D(()), D((NI,)),
            D(()), D((S,)), D(()), D((S,)), D((S,)), D(()), D((S,)), D((S,)), D(()), D((NI,)),
            D(()), D((NI,)), D(()), D((NI,)),
        ],
        compiler_params=pltpu.CompilerParams(
            collective_id=0, has_side_effects=True, vmem_limit_bytes=60 * 2**20),
    )(tokens.T, gate_weight, up_weight, down_weight)
    return result.T


def solution(mesh):
    placed = (P(None, ("gx", "yz")), P("gx", "yz"), P("gx", "yz"), P("yz", "gx"))
    return jax.shard_map(
        body, mesh=mesh, in_specs=placed, out_specs=P(None, ("gx", "yz")), check_vma=False
    )
```

```python
import jax
import jax.numpy as jnp
from jax import lax
from jax.experimental import pallas as pl
from jax.experimental.pallas import tpu as pltpu
from jax.sharding import PartitionSpec as P

BF = jnp.bfloat16
F32 = jnp.float32
MESH = pl.DeviceIdType.MESH

ROWS = 768
R = 128
NI = ROWS // R
NJ = 3
S = NI * NJ
Q = R // 4
K = 1536
FF = 2304
FB = FF // 2 // NJ
XB = 96
HB = XB // 2

LAGS = 2, 4, 6, 8, 9, 13, 16
LC, LD, LE, LF, LG, LZ, LO = LAGS
LS = 2
NT = 2
DIRECT = S - 3


OTHERS = sorted(((kz, kx) for kz in range(4) for kx in range(4) if kz or kx), key=lambda k: -sum(min(v, 4 - v) for v in k))


def kernel(tok_hbm, wg_hbm, wu_hbm, wd_hbm, out,
           wgu, wd, tok, tokr, sibs, sibr, par, own, yr, hid, terms, r1, r2,
           w_sem, wd_sem, tl_sem, t1_s, t1_r, t2_s, t2_r,
           d_s, d_r, y_s, c_r, e_r, h_s, h_r, hf_r, f_s, f_r, z1_s, z1_r, z2_s, z2_r, l_s):
    g = lax.axis_index("gx")
    s_ = lax.axis_index("yz")
    y, c = g // 2, g % 2
    z, x = s_ // 4, s_ % 4

    def m4(v):
        return lax.rem(v, 4)

    sib_dev = (y * 2 + 1 - c, s_)
    yp, ym, yo = (m4(y + 1) * 2 + c, s_), (m4(y + 3) * 2 + c, s_), (m4(y + 2) * 2 + c, s_)

    def at_z(k):
        return (g, m4(z + k) * 4 + x)

    def at_x(k):
        return (g, z * 4 + m4(x + k))

    def at_zx(kz, kx):
        return (g, m4(z + kz) * 4 + m4(x + kx))

    def rc(src, dst, ss, rs, dev):
        return pltpu.make_async_remote_copy(
            src_ref=src, dst_ref=dst, send_sem=ss, recv_sem=rs,
            device_id=dev, device_id_type=MESH)

    def arrived(ref, sem):
        rc(ref, ref, y_s, sem, sib_dev).wait_recv()

    def sent(ref, sem):
        rc(ref, ref, sem, d_r.at[0], sib_dev).wait_send()

    def rows(q, n):
        return pl.ds(pl.multiple_of(q * n, 16), n)

    def lanes(b, n):
        return pl.ds(pl.multiple_of(b * n, 128), n)

    A, B = pl.ds(0, HB), pl.ds(HB, HB)

    barrier = pltpu.get_barrier_semaphore()
    partners = [sib_dev, yp, ym, yo] + [at_zx(kz, kx) for kz, kx in OTHERS]
    for dev in partners:
        pl.semaphore_signal(barrier, inc=1, device_id=dev, device_id_type=MESH)

    def b_sib(j):
        return (1 - c) * NJ + j

    def b_own(j):
        return c * NJ + j

    def tl_copy(i):
        return pltpu.make_async_copy(tok_hbm.at[:, pl.ds(i * R, R)], tok.at[i, z, x], tl_sem)

    for i in range(NI):
        tl_copy(i).start()

    def w_copies(b):
        cols = lanes(b, FB)
        return (pltpu.make_async_copy(wg_hbm.at[:, cols], wgu.at[b, :, pl.ds(0, FB)], w_sem.at[b]),
                pltpu.make_async_copy(wu_hbm.at[:, cols], wgu.at[b, :, pl.ds(FB, FB)], w_sem.at[b]))

    def w_arrived(b):
        pltpu.make_async_copy(wgu.at[b], wgu.at[b], w_sem.at[b]).wait()

    wd_copy = pltpu.make_async_copy(wd_hbm, wd, wd_sem)

    def weights_start():
        for j in range(NJ):
            for b in (b_sib(j), b_own(j)):
                for cp in w_copies(b):
                    cp.start()
        wd_copy.start()

    def t1_copy(i, h, k):
        half = A if h == 0 else B
        return rc(tok.at[i, z, x, half], tok.at[i, z, x, half], t1_s, t1_r.at[i],
                  at_x(k) if h == 0 else at_z(k))

    def t2_copy(i, h, k):
        blk = tok.at[i, z, :, A] if h == 0 else tok.at[i, :, x, B]
        return rc(blk, blk, t2_s, t2_r.at[i], at_z(k) if h == 0 else at_x(k))

    def t0_start():
        for kz, kx in OTHERS:
            rc(tok.at[0, z, x], tok.at[0, z, x], l_s, t2_r.at[0], at_zx(kz, kx)).start()

    BOTH = [(h, k) for k in (2, 1, 3) for h in (0, 1)]

    def tok_first(i):
        for h, k in BOTH:
            t1_copy(i, h, k).start()

    def tok_second(i):
        arrived(r2.at[i], t1_r.at[i])
        for h, k in BOTH:
            t2_copy(i, h, k).start()

    def tok_ready(i):
        @pl.when(i == 0)
        def _():
            arrived(r2.at[pl.ds(0, 5)], t2_r.at[0])

        @pl.when(i > 0)
        def _():
            arrived(r1.at[i], t2_r.at[i])

        tokr[i % 2] = tok[i].reshape(K, R).T

    def entry_barrier():
        pl.semaphore_wait(barrier, len(partners))

    def entry_own():
        pltpu.make_async_copy(tok.at[:, 0, 0], tok.at[:, 0, 0], tl_sem).wait()

    entry_own()
    entry_barrier()
    t0_start()
    weights_start()
    tok_first(1)
    tok_second(1)

    def d_copy(s):
        return rc(sibs.at[s], sibr.at[s], d_s, d_r.at[s], sib_dev)

    def stage_sib(s):
        i, j = s // NJ, s % NJ

        @pl.when(j == 0)
        def _():
            tok_ready(i)

        @pl.when(i == 0)
        def _():
            w_arrived(b_sib(j))

        sibs[s] = jnp.dot(tokr[i % 2], wgu[b_sib(j)], preferred_element_type=F32).astype(BF)
        d_copy(s).start()

        @pl.when((j == 0) & (i + 1 < NI))
        def _():
            @pl.when(i > 0)
            def _():
                tok_second(i + 1)

            @pl.when(i + 2 < NI)
            def _():
                tok_first(i + 2)

    def stage_own(s):
        i, j = s // NJ, s % NJ

        @pl.when(i == 0)
        def _():
            w_arrived(b_own(j))

        own[...] = jnp.dot(tokr[i % 2], wgu[b_own(j)], preferred_element_type=F32)

    G, U = pl.ds(0, FB), pl.ds(FB, FB)

    def y_copy(s, n):
        q, cols, dev = ((2, G, yp), (2, U, ym), (1, U, yp), (3, G, ym), (1, G, yp), (3, U, ym))[n]
        return rc(par.at[s, rows(m4(y + q), Q), cols], yr.at[s, n], y_s, (c_r if n < 2 else e_r).at[s], dev)

    def stage_merge(s):
        arrived(sibr.at[s], d_r.at[s])
        par[s] = (own[...] + sibr[s].astype(F32)).astype(BF)
        for n in range(4):
            y_copy(s, n).start()

    def stage_c(s):
        arrived(yr.at[s, pl.ds(0, 2)], c_r.at[s])
        rr = rows(m4(y + 1), Q)
        par[s, rr, G] = (par[s, rr, G].astype(F32) + yr[s, 0].astype(F32)).astype(BF)
        y_copy(s, 4).start()
        rr = rows(m4(y + 3), Q)
        par[s, rr, U] = (par[s, rr, U].astype(F32) + yr[s, 1].astype(F32)).astype(BF)
        y_copy(s, 5).start()

    def h_block(s, k):
        i, j = s // NJ, s % NJ
        return hid.at[i, rows(m4(y + k), Q), lanes(b_own(j), FB)]

    def h_copy(s, d):
        blk = h_block(s, 0)
        return rc(blk, blk, h_s, h_r.at[s], yp if d == 0 else ym)

    def hf_copy(s, d):
        blk = h_block(s, 3 if d == 0 else 1)
        return rc(blk, blk, h_s, hf_r.at[s], yp if d == 0 else ym)

    def ho_copy(s):
        blk = h_block(s, 0)
        return rc(blk, blk, h_s, hf_r.at[s], yo)

    def stage_d(s):
        i, j = s // NJ, s % NJ
        arrived(yr.at[s, pl.ds(2, 4)], e_r.at[s])
        rr = rows(y, Q)
        gate = par[s, rr, G].astype(F32) + (yr[s, 3].astype(F32) + yr[s, 4].astype(F32))
        up = par[s, rr, U].astype(F32) + (yr[s, 2].astype(F32) + yr[s, 5].astype(F32))
        hid[i, rr, lanes(b_own(j), FB)] = (gate / (1.0 + jnp.exp(-gate)) * up).astype(BF)
        @pl.when(s >= DIRECT)
        def _():
            ho_copy(s).start()

        for d in range(2):
            h_copy(s, d).start()

    def stage_e(s):
        arrived(yr.at[s, pl.ds(0, 2)], h_r.at[s])

        @pl.when((s < DIRECT) & (s % 2 == 0))
        def _():
            hf_copy(s, 0).start()

        @pl.when((s < DIRECT) & (s % 2 == 1))
        def _():
            hf_copy(s, 1).start()

    def f_copy(s, half):
        i, j = s // NJ, s % NJ
        blk = hid.at[i, :, lanes(half * NJ + j, FB)]
        return rc(blk, blk, f_s, f_r.at[i], sib_dev)

    def stage_f(s):
        arrived(yr.at[s, 0], hf_r.at[s])
        f_copy(s, c).start()

    def z1_copy(i, h, k):
        if h == 0:
            src, dev = terms.at[i, m4(z + k), :, A], at_z(k)
        else:
            src, dev = terms.at[i, :, m4(x + k), B], at_x(k)
        return rc(src, r1.at[i, h, k - 1], z1_s, z1_r.at[i], dev)

    def z2_copy(i, h, k):
        if h == 0:
            src, dev = terms.at[i, z, m4(x + k), A], at_x(k)
        else:
            src, dev = terms.at[i, m4(z + k), x, B], at_z(k)
        return rc(src, r2.at[i, h, k - 1], z2_s, z2_r.at[i], dev)

    def stage_g(i):
        @pl.when(i == 0)
        def _():
            wd_copy.wait()

        arrived(hid.at[i, :, pl.ds(0, FF // 2)], f_r.at[i])
        mine = z // 2
        for n in range(2):
            p = mine if n else 1 - mine
            res = jnp.dot(hid[i], wd[:, lanes(p, K // 2)], preferred_element_type=F32).astype(BF)
            terms[i, pl.ds(2 * p, 2)] = res.T.reshape(2, 4, XB, R)
        for h, k in BOTH:
            z1_copy(i, h, k).start()

    def stage_z(i):
        arrived(r1.at[i], z1_r.at[i])
        for h in (0, 1):
            v = r1[i, h, 0].astype(F32) + r1[i, h, 1].astype(F32) + r1[i, h, 2].astype(F32)
            if h == 0:
                terms[i, z, :, A] = (terms[i, z, :, A].astype(F32) + v).astype(BF)
            else:
                terms[i, :, x, B] = (terms[i, :, x, B].astype(F32) + v).astype(BF)
            for k in (2, 1, 3):
                z2_copy(i, h, k).start()

    def stage_out(i):
        cols = lanes(i, R)
        arrived(r2.at[i], z2_r.at[i])
        for h, half in ((0, A), (1, B)):
            v = terms[i, z, x, half].astype(F32)
            for k in (0, 1, 2):
                v = v + r2[i, h, k].astype(F32)
            out[half, cols] = v.astype(BF)

    def step(u, _):
        t = u - LS

        @pl.when((t >= 0) & (t < S))
        def _():
            stage_own(t)
            stage_merge(t)

        @pl.when(t + LS < S)
        def _():
            stage_sib(t + LS)

        def lag(n, f):
            s = t - n

            @pl.when((s >= 0) & (s < S))
            def _():
                f(s)

        def lag_i(n, f, most):
            s = t - n

            @pl.when((s >= 0) & (s < most * NJ) & (lax.rem(s + 2 * S, NJ) == NJ - 1))
            def _():
                f(s // NJ)

        lag(LC, stage_c)
        lag(LD, stage_d)
        lag(LE, stage_e)
        lag(LF, stage_f)
        lag_i(LG, stage_g, NI - 2)
        lag_i(LZ, stage_z, NT)
        lag_i(LO, stage_out, NT)
        return 0

    lax.fori_loop(0, S + LD + LS, step, 0)
    for s in range(S + LD - LF, S + LD - LE):
        stage_f(s)
    for s in range(S + LD - LE, S - 1):
        stage_e(s)
        stage_f(s)

    def last(n, _):
        i = NI - 2 + n

        @pl.when(n == 1)
        def _():
            stage_e(S - 1)
            stage_f(S - 1)

        stage_g(i)
        return 0

    lax.fori_loop(0, 2, last, 0)
    for i in range(NT, NI):
        stage_z(i)
    for i in range(NT, NI):
        stage_out(i)

    def entry_sent():
        for ref, sem in ((r2.at[pl.ds(1, NI - 1)], t1_s), (r1.at[pl.ds(1, NI - 1)], t2_s), (r2.at[pl.ds(0, 5)], l_s), (sibs, d_s), (yr, y_s), (yr.at[:, pl.ds(0, 3)], h_s),
                         (hid.at[:, :, pl.ds(0, FF // 2)], f_s), (r1, z1_s), (r2, z2_s)):
            sent(ref, sem)

    entry_sent()


def body(tokens, gate_weight, up_weight, down_weight):
    V = pltpu.VMEM
    D = pltpu.SemaphoreType.DMA
    result = pl.pallas_call(
        kernel,
        out_shape=jax.ShapeDtypeStruct((XB, ROWS), BF),
        in_specs=[pl.BlockSpec(memory_space=pl.ANY)] * 4,
        out_specs=pl.BlockSpec(memory_space=V),
        scratch_shapes=[
            V((2 * NJ, K, 2 * FB), BF),
            V((FF, K), BF),
            V((NI, 4, 4, XB, R), BF),
            V((2, R, K), BF),
            V((S, R, 2 * FB), BF),
            V((S, R, 2 * FB), BF),
            V((S, R, 2 * FB), BF),
            V((R, 2 * FB), F32),
            V((S, 6, Q, FB), BF),
            V((NI, R, FF), BF),
            V((NI, 4, 4, XB, R), BF),
            V((NI, 2, 3, 4, HB, R), BF),
            V((NI, 2, 3, HB, R), BF),
            D((2 * NJ,)), D(()), D(()),
            D(()), D((NI,)), D(()), D((NI,)),
            D(()), D((S,)), D(()), D((S,)), D((S,)), D(()), D((S,)), D((S,)), D(()), D((NI,)),
            D(()), D((NI,)), D(()), D((NI,)), D(()),
        ],
        compiler_params=pltpu.CompilerParams(
            collective_id=0, has_side_effects=True, vmem_limit_bytes=60 * 2**20),
    )(tokens.T, gate_weight, up_weight, down_weight)
    return result.T


def solution(mesh):
    placed = (P(None, ("gx", "yz")), P("gx", "yz"), P("gx", "yz"), P("yz", "gx"))
    return jax.shard_map(
        body, mesh=mesh, in_specs=placed, out_specs=P(None, ("gx", "yz")), check_vma=False
    )
```

```python
import jax
import jax.numpy as jnp
from jax import lax
from jax.experimental import pallas as pl
from jax.experimental.pallas import tpu as pltpu
from jax.sharding import PartitionSpec as P

BF = jnp.bfloat16
F32 = jnp.float32
MESH = pl.DeviceIdType.MESH

ROWS = 768
R = 128
NI = ROWS // R
NJ = 3
S = NI * NJ
Q = R // 4
K = 1536
FF = 2304
FB = FF // 2 // NJ
XB = 96
HB = XB // 2

LAGS = 2, 4, 6, 8, 9, 13, 16
LC, LD, LE, LF, LG, LZ, LO = LAGS
LS = 2
NS = 9
NT = 2
DIRECT = S - 3


OTHERS = sorted(((kz, kx) for kz in range(4) for kx in range(4) if kz or kx), key=lambda k: -sum(min(v, 4 - v) for v in k))


def kernel(tok_hbm, wg_hbm, wu_hbm, wd_hbm, out,
           wgu, wd, tok, tokr, sibs, sibr, par, own, yr, hid, terms, r1, r2,
           w_sem, wd_sem, tl_sem, t1_s, t1_r, t2_s, t2_r,
           d_s, d_r, y_s, c_r, e_r, h_s, h_r, hf_r, f_s, f_r, z1_s, z1_r, z2_s, z2_r, l_s):
    g = lax.axis_index("gx")
    s_ = lax.axis_index("yz")
    y, c = g // 2, g % 2
    z, x = s_ // 4, s_ % 4

    def m4(v):
        return lax.rem(v, 4)

    sib_dev = (y * 2 + 1 - c, s_)
    yp, ym, yo = (m4(y + 1) * 2 + c, s_), (m4(y + 3) * 2 + c, s_), (m4(y + 2) * 2 + c, s_)

    def at_z(k):
        return (g, m4(z + k) * 4 + x)

    def at_x(k):
        return (g, z * 4 + m4(x + k))

    def at_zx(kz, kx):
        return (g, m4(z + kz) * 4 + m4(x + kx))

    def rc(src, dst, ss, rs, dev):
        return pltpu.make_async_remote_copy(
            src_ref=src, dst_ref=dst, send_sem=ss, recv_sem=rs,
            device_id=dev, device_id_type=MESH)

    def arrived(ref, sem):
        rc(ref, ref, y_s, sem, sib_dev).wait_recv()

    def sent(ref, sem):
        rc(ref, ref, sem, d_r.at[0], sib_dev).wait_send()

    def rows(q, n):
        return pl.ds(pl.multiple_of(q * n, 16), n)

    def lanes(b, n):
        return pl.ds(pl.multiple_of(b * n, 128), n)

    A, B = pl.ds(0, HB), pl.ds(HB, HB)

    barrier = pltpu.get_barrier_semaphore()
    partners = [sib_dev, yp, ym, yo] + [at_zx(kz, kx) for kz, kx in OTHERS]
    for dev in partners:
        pl.semaphore_signal(barrier, inc=1, device_id=dev, device_id_type=MESH)

    def b_sib(j):
        return (1 - c) * NJ + j

    def b_own(j):
        return c * NJ + j

    def tl_copy(i):
        return pltpu.make_async_copy(tok_hbm.at[:, pl.ds(i * R, R)], tok.at[i, z, x], tl_sem)

    for i in range(NI):
        tl_copy(i).start()

    def w_copies(b):
        cols = lanes(b, FB)
        return (pltpu.make_async_copy(wg_hbm.at[:, cols], wgu.at[b, :, pl.ds(0, FB)], w_sem.at[b]),
                pltpu.make_async_copy(wu_hbm.at[:, cols], wgu.at[b, :, pl.ds(FB, FB)], w_sem.at[b]))

    def w_arrived(b):
        pltpu.make_async_copy(wgu.at[b], wgu.at[b], w_sem.at[b]).wait()

    wd_copy = pltpu.make_async_copy(wd_hbm, wd, wd_sem)

    def weights_start(some):
        for j in some:
            for b in (b_sib(j), b_own(j)):
                for cp in w_copies(b):
                    cp.start()
        if NJ - 1 in some:
            wd_copy.start()

    def t1_copy(i, h, k):
        half = A if h == 0 else B
        return rc(tok.at[i, z, x, half], tok.at[i, z, x, half], t1_s, t1_r.at[i],
                  at_x(k) if h == 0 else at_z(k))

    def t2_copy(i, h, k):
        blk = tok.at[i, z, :, A] if h == 0 else tok.at[i, :, x, B]
        return rc(blk, blk, t2_s, t2_r.at[i], at_z(k) if h == 0 else at_x(k))

    def t0_start():
        for kz, kx in OTHERS:
            rc(tok.at[0, z, x], tok.at[0, z, x], l_s, t2_r.at[0], at_zx(kz, kx)).start()

    BOTH = [(h, k) for k in (2, 1, 3) for h in (0, 1)]

    def tok_first(i):
        for h, k in BOTH:
            t1_copy(i, h, k).start()

    def tok_second(i):
        arrived(r2.at[i], t1_r.at[i])
        for h, k in BOTH:
            t2_copy(i, h, k).start()

    def tok_ready(i):
        @pl.when(i == 0)
        def _():
            arrived(r2.at[pl.ds(0, 5)], t2_r.at[0])

        @pl.when(i > 0)
        def _():
            arrived(r1.at[i], t2_r.at[i])

        tokr[i % 2] = tok[i].reshape(K, R).T

    def entry_barrier():
        pl.semaphore_wait(barrier, len(partners))

    def entry_own():
        pltpu.make_async_copy(tok.at[:, 0, 0], tok.at[:, 0, 0], tl_sem).wait()

    entry_own()
    entry_barrier()
    weights_start(range(1))
    t0_start()
    tok_first(1)
    weights_start(range(1, NJ))
    tok_second(1)

    def d_copy(s):
        return rc(sibs.at[s], sibr.at[s], d_s, d_r.at[s % NS], sib_dev)

    def stage_sib(s):
        i, j = s // NJ, s % NJ

        @pl.when(j == 0)
        def _():
            tok_ready(i)

        @pl.when(i == 0)
        def _():
            w_arrived(b_sib(j))

        sibs[s] = jnp.dot(tokr[i % 2], wgu[b_sib(j)], preferred_element_type=F32).astype(BF)
        d_copy(s).start()

        @pl.when((j == 0) & (i + 1 < NI))
        def _():
            @pl.when(i > 0)
            def _():
                tok_second(i + 1)

            @pl.when(i + 2 < NI)
            def _():
                tok_first(i + 2)

    def stage_own(s):
        i, j = s // NJ, s % NJ

        @pl.when(i == 0)
        def _():
            w_arrived(b_own(j))

        own[...] = jnp.dot(tokr[i % 2], wgu[b_own(j)], preferred_element_type=F32)

    def y_copy(s, n):
        ahead = 1 + 2 * (s % 2)
        q, to = ((2, ahead), (4 - ahead, 4 - ahead), (ahead, ahead))[n]
        return rc(par.at[s, rows(m4(y + q), Q)], yr.at[s, n], y_s, (e_r if n else c_r).at[s % NS], (m4(y + to) * 2 + c, s_))

    def stage_merge(s):
        arrived(sibr.at[s], d_r.at[s % NS])
        par[s] = (own[...] + sibr[s].astype(F32)).astype(BF)
        for n in range(2):
            y_copy(s, n).start()

    def stage_c(s):
        arrived(yr.at[s, 0], c_r.at[s % NS])
        rr = rows(m4(y + 1 + 2 * (s % 2)), Q)
        par[s, rr, :] = (par[s, rr, :].astype(F32) + yr[s, 0].astype(F32)).astype(BF)
        y_copy(s, 2).start()

    def h_block(s, k):
        i, j = s // NJ, s % NJ
        return hid.at[i, rows(m4(y + k), Q), lanes(b_own(j), FB)]

    def h_copy(s, d):
        blk = h_block(s, 0)
        return rc(blk, blk, h_s, h_r.at[s % NS], yp if d == 0 else ym)

    def hf_copy(s, d):
        blk = h_block(s, 3 if d == 0 else 1)
        return rc(blk, blk, h_s, hf_r.at[s], yp if d == 0 else ym)

    def ho_copy(s):
        blk = h_block(s, 0)
        return rc(blk, blk, h_s, hf_r.at[s], yo)

    def stage_d(s):
        i, j = s // NJ, s % NJ
        arrived(yr.at[s, pl.ds(1, 2)], e_r.at[s % NS])
        rr = rows(y, Q)
        both = par[s, rr, :].astype(F32) + (yr[s, 1].astype(F32) + yr[s, 2].astype(F32))
        gate, up = both[:, :FB], both[:, FB:]
        hid[i, rr, lanes(b_own(j), FB)] = (gate / (1.0 + jnp.exp(-gate)) * up).astype(BF)
        @pl.when(s >= DIRECT)
        def _():
            ho_copy(s).start()

        for d in range(2):
            h_copy(s, d).start()

    def stage_e(s):
        arrived(yr.at[s, 0], h_r.at[s % NS])

        @pl.when((s < DIRECT) & (s % 2 == 1))
        def _():
            hf_copy(s, 0).start()

        @pl.when((s < DIRECT) & (s % 2 == 0))
        def _():
            hf_copy(s, 1).start()

    def f_copy(s, half):
        i, j = s // NJ, s % NJ
        blk = hid.at[i, :, lanes(half * NJ + j, FB)]
        return rc(blk, blk, f_s, f_r.at[i], sib_dev)

    def stage_f(s):
        arrived(yr.at[s, 0, :, pl.ds(0, FB)], hf_r.at[s])
        f_copy(s, c).start()

    def z1_copy(i, h, k):
        if h == 0:
            src, dev = terms.at[i, m4(z + k), :, A], at_z(k)
        else:
            src, dev = terms.at[i, :, m4(x + k), B], at_x(k)
        return rc(src, r1.at[i, h, k - 1], z1_s, z1_r.at[i], dev)

    def z2_copy(i, h, k):
        if h == 0:
            src, dev = terms.at[i, z, m4(x + k), A], at_x(k)
        else:
            src, dev = terms.at[i, m4(z + k), x, B], at_z(k)
        return rc(src, r2.at[i, h, k - 1], z2_s, z2_r.at[i], dev)

    def stage_g(i):
        @pl.when(i == 0)
        def _():
            wd_copy.wait()

        arrived(hid.at[i, :, pl.ds(0, FF // 2)], f_r.at[i])
        mine = z // 2
        for n in range(2):
            p = mine if n else 1 - mine
            res = jnp.dot(hid[i], wd[:, lanes(p, K // 2)], preferred_element_type=F32).astype(BF)
            terms[i, pl.ds(2 * p, 2)] = res.T.reshape(2, 4, XB, R)
        for h, k in BOTH:
            z1_copy(i, h, k).start()

    def stage_z(i):
        arrived(r1.at[i], z1_r.at[i])
        for h in (0, 1):
            v = r1[i, h, 0].astype(F32) + r1[i, h, 1].astype(F32) + r1[i, h, 2].astype(F32)
            if h == 0:
                terms[i, z, :, A] = (terms[i, z, :, A].astype(F32) + v).astype(BF)
            else:
                terms[i, :, x, B] = (terms[i, :, x, B].astype(F32) + v).astype(BF)
            for k in (2, 1, 3):
                z2_copy(i, h, k).start()

    def stage_out(i):
        cols = lanes(i, R)
        arrived(r2.at[i], z2_r.at[i])
        for h, half in ((0, A), (1, B)):
            v = terms[i, z, x, half].astype(F32)
            for k in (0, 1, 2):
                v = v + r2[i, h, k].astype(F32)
            out[half, cols] = v.astype(BF)

    def step(u, _):
        t = u - LS

        @pl.when((t >= 0) & (t < S))
        def _():
            stage_own(t)
            stage_merge(t)

        @pl.when(t + LS < S)
        def _():
            stage_sib(t + LS)

        def lag(n, f):
            s = t - n

            @pl.when((s >= 0) & (s < S))
            def _():
                f(s)

        def lag_i(n, f, most):
            s = t - n

            @pl.when((s >= 0) & (s < most * NJ) & (lax.rem(s + 2 * S, NJ) == NJ - 1))
            def _():
                f(s // NJ)

        lag(LC, stage_c)
        lag(LD, stage_d)
        lag(LE, stage_e)
        lag(LF, stage_f)
        lag_i(LG, stage_g, NI - 2)
        lag_i(LZ, stage_z, NT + 1)
        lag_i(LO, stage_out, NT)
        return 0

    lax.fori_loop(0, S + LD + LS, step, 0)
    for s in range(S + LD - LF, S + LD - LE):
        stage_f(s)
    for s in range(S + LD - LE, S - 1):
        stage_e(s)
        stage_f(s)

    def last(n, _):
        i = NI - 2 + n

        @pl.when(n == 1)
        def _():
            stage_e(S - 1)
            stage_f(S - 1)

        stage_g(i)
        return 0

    lax.fori_loop(0, 2, last, 0)
    for i in range(NT + 1, NI):
        stage_z(i)
    for i in range(NT, NI):
        stage_out(i)

    def entry_sent():
        for ref, sem in ((r2.at[pl.ds(1, NI - 1)], t1_s), (r1.at[pl.ds(1, NI - 1)], t2_s), (r2.at[pl.ds(0, 5)], l_s), (sibs, d_s), (yr, y_s), (yr.at[:, :, :, pl.ds(0, FB)], h_s),
                         (hid.at[:, :, pl.ds(0, FF // 2)], f_s), (r1, z1_s), (r2, z2_s)):
            sent(ref, sem)

    entry_sent()


def body(tokens, gate_weight, up_weight, down_weight):
    V = pltpu.VMEM
    D = pltpu.SemaphoreType.DMA
    result = pl.pallas_call(
        kernel,
        out_shape=jax.ShapeDtypeStruct((XB, ROWS), BF),
        in_specs=[pl.BlockSpec(memory_space=pl.ANY)] * 4,
        out_specs=pl.BlockSpec(memory_space=V),
        scratch_shapes=[
            V((2 * NJ, K, 2 * FB), BF),
            V((FF, K), BF),
            V((NI, 4, 4, XB, R), BF),
            V((2, R, K), BF),
            V((S, R, 2 * FB), BF),
            V((S, R, 2 * FB), BF),
            V((S, R, 2 * FB), BF),
            V((R, 2 * FB), F32),
            V((S, 3, Q, 2 * FB), BF),
            V((NI, R, FF), BF),
            V((NI, 4, 4, XB, R), BF),
            V((NI, 2, 3, 4, HB, R), BF),
            V((NI, 2, 3, HB, R), BF),
            D((2 * NJ,)), D(()), D(()),
            D(()), D((NI,)), D(()), D((NI,)),
            D(()), D((NS,)), D(()), D((NS,)), D((NS,)), D(()), D((NS,)), D((S,)), D(()), D((NI,)),
            D(()), D((NI,)), D(()), D((NI,)), D(()),
        ],
        compiler_params=pltpu.CompilerParams(
            collective_id=0, has_side_effects=True, vmem_limit_bytes=60 * 2**20),
    )(tokens.T, gate_weight, up_weight, down_weight)
    return result.T


def solution(mesh):
    placed = (P(None, ("gx", "yz")), P("gx", "yz"), P("gx", "yz"), P("yz", "gx"))
    return jax.shard_map(
        body, mesh=mesh, in_specs=placed, out_specs=P(None, ("gx", "yz")), check_vma=False
    )
```

```python
import jax
import jax.numpy as jnp
from jax import lax
from jax.experimental import pallas as pl
from jax.experimental.pallas import tpu as pltpu
from jax.sharding import PartitionSpec as P

BF = jnp.bfloat16
F32 = jnp.float32
MESH = pl.DeviceIdType.MESH

ROWS = 768
R = 128
NI = ROWS // R
NJ = 3
S = NI * NJ
Q = R // 4
K = 1536
FF = 2304
FB = FF // 2 // NJ
XB = 96
HB = XB // 2

LAGS = 2, 4, 6, 8, 9, 13, 16
LC, LD, LE, LF, LG, LZ, LO = LAGS
LS = 2
NS = 9
NT = 2
DIRECT = S - 3


OTHERS = sorted(((kz, kx) for kz in range(4) for kx in range(4) if kz or kx), key=lambda k: -sum(min(v, 4 - v) for v in k))


def kernel(tok_hbm, wg_hbm, wu_hbm, wd_hbm, out,
           wgu, wd, tok, tokr, sibs, sibr, par, own, acc, yr, hid, terms, r1, r2,
           w_sem, wd_sem, tl_sem, t1_s, t1_r, t2_s, t2_r,
           d_s, d_r, y_s, c_r, e_r, h_s, h_r, hf_r, f_s, f_r, z1_s, z1_r, z2_s, z2_r, l_s):
    g = lax.axis_index("gx")
    s_ = lax.axis_index("yz")
    y, c = g // 2, g % 2
    z, x = s_ // 4, s_ % 4

    def m4(v):
        return lax.rem(v, 4)

    sib_dev = (y * 2 + 1 - c, s_)
    yp, ym, yo = (m4(y + 1) * 2 + c, s_), (m4(y + 3) * 2 + c, s_), (m4(y + 2) * 2 + c, s_)

    def at_z(k):
        return (g, m4(z + k) * 4 + x)

    def at_x(k):
        return (g, z * 4 + m4(x + k))

    def at_zx(kz, kx):
        return (g, m4(z + kz) * 4 + m4(x + kx))

    def rc(src, dst, ss, rs, dev):
        return pltpu.make_async_remote_copy(
            src_ref=src, dst_ref=dst, send_sem=ss, recv_sem=rs,
            device_id=dev, device_id_type=MESH)

    def arrived(ref, sem):
        rc(ref, ref, y_s, sem, sib_dev).wait_recv()

    def sent(ref, sem):
        rc(ref, ref, sem, d_r.at[0], sib_dev).wait_send()

    def rows(q, n):
        return pl.ds(pl.multiple_of(q * n, 16), n)

    def lanes(b, n):
        return pl.ds(pl.multiple_of(b * n, 128), n)

    A, B = pl.ds(0, HB), pl.ds(HB, HB)

    barrier = pltpu.get_barrier_semaphore()
    partners = [sib_dev, yp, ym, yo] + [at_zx(kz, kx) for kz, kx in OTHERS]
    for dev in partners:
        pl.semaphore_signal(barrier, inc=1, device_id=dev, device_id_type=MESH)

    def b_sib(j):
        return (1 - c) * NJ + j

    def b_own(j):
        return c * NJ + j

    def tl_copy(i):
        return pltpu.make_async_copy(tok_hbm.at[:, pl.ds(i * R, R)], tok.at[i, z, x], tl_sem)

    for i in range(NI):
        tl_copy(i).start()

    def w_copies(b):
        cols = lanes(b, FB)
        return (pltpu.make_async_copy(wg_hbm.at[:, cols], wgu.at[b, :, pl.ds(0, FB)], w_sem.at[b]),
                pltpu.make_async_copy(wu_hbm.at[:, cols], wgu.at[b, :, pl.ds(FB, FB)], w_sem.at[b]))

    def w_arrived(b):
        pltpu.make_async_copy(wgu.at[b], wgu.at[b], w_sem.at[b]).wait()

    wd_copy = pltpu.make_async_copy(wd_hbm, wd, wd_sem)

    def weights_start(some):
        for j in some:
            for b in (b_sib(j), b_own(j)):
                for cp in w_copies(b):
                    cp.start()
        if NJ - 1 in some:
            wd_copy.start()

    def t1_copy(i, h, k):
        half = A if h == 0 else B
        return rc(tok.at[i, z, x, half], tok.at[i, z, x, half], t1_s, t1_r.at[i],
                  at_x(k) if h == 0 else at_z(k))

    def t2_copy(i, h, k):
        blk = tok.at[i, z, :, A] if h == 0 else tok.at[i, :, x, B]
        return rc(blk, blk, t2_s, t2_r.at[i], at_z(k) if h == 0 else at_x(k))

    def t0_start():
        for kz, kx in OTHERS:
            rc(tok.at[0, z, x], tok.at[0, z, x], l_s, t2_r.at[0], at_zx(kz, kx)).start()

    BOTH = [(h, k) for k in (2, 1, 3) for h in (0, 1)]

    def tok_first(i):
        for h, k in BOTH:
            t1_copy(i, h, k).start()

    def tok_second(i):
        arrived(r2.at[i], t1_r.at[i])
        for h, k in BOTH:
            t2_copy(i, h, k).start()

    def tok_ready(i):
        @pl.when(i == 0)
        def _():
            arrived(r2.at[pl.ds(0, 5)], t2_r.at[0])

        @pl.when(i > 0)
        def _():
            arrived(r1.at[i], t2_r.at[i])

        tokr[i % 2] = tok[i].reshape(K, R).T

    def entry_barrier():
        pl.semaphore_wait(barrier, len(partners))

    def entry_own():
        pltpu.make_async_copy(tok.at[:, 0, 0], tok.at[:, 0, 0], tl_sem).wait()

    entry_own()
    entry_barrier()
    weights_start(range(1))
    t0_start()
    tok_first(1)
    weights_start(range(1, NJ))
    tok_second(1)

    def d_copy(s):
        return rc(sibs.at[s], sibr.at[s], d_s, d_r.at[s % NS], sib_dev)

    def stage_sib(s):
        i, j = s // NJ, s % NJ

        @pl.when(j == 0)
        def _():
            tok_ready(i)

        @pl.when(i == 0)
        def _():
            w_arrived(b_sib(j))

        sibs[s] = jnp.dot(tokr[i % 2], wgu[b_sib(j)], preferred_element_type=F32).astype(BF)
        d_copy(s).start()

        @pl.when((j == 0) & (i + 1 < NI))
        def _():
            @pl.when(i > 0)
            def _():
                tok_second(i + 1)

            @pl.when(i + 2 < NI)
            def _():
                tok_first(i + 2)

    def stage_own(s):
        i, j = s // NJ, s % NJ

        @pl.when(i == 0)
        def _():
            w_arrived(b_own(j))

        own[...] = jnp.dot(tokr[i % 2], wgu[b_own(j)], preferred_element_type=F32)

    def y_copy(s, n):
        ahead = 1 + 2 * (s % 2)
        q, to = ((2, ahead), (4 - ahead, 4 - ahead), (ahead, ahead))[n]
        return rc(par.at[s, rows(m4(y + q), Q)], yr.at[s, n], y_s, (e_r if n else c_r).at[s % NS], (m4(y + to) * 2 + c, s_))

    def stage_merge(s):
        arrived(sibr.at[s], d_r.at[s % NS])
        par[s] = (own[...] + sibr[s].astype(F32)).astype(BF)
        for n in range(2):
            y_copy(s, n).start()

    def stage_c(s):
        arrived(yr.at[s, 0], c_r.at[s % NS])
        rr = rows(m4(y + 1 + 2 * (s % 2)), Q)
        par[s, rr, :] = (par[s, rr, :].astype(F32) + yr[s, 0].astype(F32)).astype(BF)
        y_copy(s, 2).start()

    def h_block(s, k):
        i, j = s // NJ, s % NJ
        return hid.at[i, rows(m4(y + k), Q), lanes(b_own(j), FB)]

    def h_copy(s, d):
        blk = h_block(s, 0)
        return rc(blk, blk, h_s, h_r.at[s % NS], yp if d == 0 else ym)

    def hf_copy(s, d):
        blk = h_block(s, 3 if d == 0 else 1)
        return rc(blk, blk, h_s, hf_r.at[s], yp if d == 0 else ym)

    def ho_copy(s):
        blk = h_block(s, 0)
        return rc(blk, blk, h_s, hf_r.at[s], yo)

    def stage_d(s):
        i, j = s // NJ, s % NJ
        arrived(yr.at[s, pl.ds(1, 2)], e_r.at[s % NS])
        rr = rows(y, Q)
        both = par[s, rr, :].astype(F32) + (yr[s, 1].astype(F32) + yr[s, 2].astype(F32))
        gate, up = both[:, :FB], both[:, FB:]
        hid[i, rr, lanes(b_own(j), FB)] = (gate / (1.0 + jnp.exp(-gate)) * up).astype(BF)
        @pl.when(s >= DIRECT)
        def _():
            ho_copy(s).start()

        for d in range(2):
            h_copy(s, d).start()

    def stage_e(s):
        arrived(yr.at[s, 0], h_r.at[s % NS])

        @pl.when((s < DIRECT) & (s % 2 == 1))
        def _():
            hf_copy(s, 0).start()

        @pl.when((s < DIRECT) & (s % 2 == 0))
        def _():
            hf_copy(s, 1).start()

    def f_copy(s, half):
        i, j = s // NJ, s % NJ
        blk = hid.at[i, :, lanes(half * NJ + j, FB)]
        return rc(blk, blk, f_s, f_r.at[i + s // (S - 1)], sib_dev)

    def stage_f(s):
        arrived(yr.at[s, 0, :, pl.ds(0, FB)], hf_r.at[s])
        f_copy(s, c).start()

    def z1_copy(i, h, k):
        if h == 0:
            src, dev = terms.at[i, m4(z + k), :, A], at_z(k)
        else:
            src, dev = terms.at[i, :, m4(x + k), B], at_x(k)
        return rc(src, r1.at[i, h, k - 1], z1_s, z1_r.at[i], dev)

    def z2_copy(i, h, k):
        if h == 0:
            src, dev = terms.at[i, z, m4(x + k), A], at_x(k)
        else:
            src, dev = terms.at[i, m4(z + k), x, B], at_z(k)
        return rc(src, r2.at[i, h, k - 1], z2_s, z2_r.at[i], dev)

    def stage_g(i):
        @pl.when(i == 0)
        def _():
            wd_copy.wait()

        arrived(hid.at[i, :, pl.ds(0, FF // 2)], f_r.at[i])
        mine = z // 2
        for n in range(2):
            p = mine if n else 1 - mine
            res = jnp.dot(hid[i], wd[:, lanes(p, K // 2)], preferred_element_type=F32).astype(BF)
            terms[i, pl.ds(2 * p, 2)] = res.T.reshape(2, 4, XB, R)
        for h, k in BOTH:
            z1_copy(i, h, k).start()

    def part(js, cols):
        i, total = NI - 1, 0.0
        for half in range(2):
            k = pl.ds((half * NJ + js[0]) * FB, len(js) * FB)
            total = total + jnp.dot(hid[i, :, k], wd[k, cols], preferred_element_type=F32)
        return total

    def stage_part():
        arrived(hid.at[NI - 1, :, pl.ds(0, (NJ - 1) * FB)], f_r.at[NI - 1])
        for n in range(2):
            cols = pl.ds(n * (K // 2), K // 2)
            acc[:, cols] = part(range(NJ - 1), cols)

    def stage_rest():
        i = NI - 1
        arrived(hid.at[i, :, pl.ds(0, FB)], f_r.at[NI])
        for n in range(2):
            cols = pl.ds(n * (K // 2), K // 2)
            res = (acc[:, cols] + part([NJ - 1], cols)).astype(BF)
            terms[i, pl.ds(2 * n, 2)] = res.T.reshape(2, 4, XB, R)
        for h, k in BOTH:
            z1_copy(i, h, k).start()

    def stage_z(i):
        arrived(r1.at[i], z1_r.at[i])
        for h in (0, 1):
            v = r1[i, h, 0].astype(F32) + r1[i, h, 1].astype(F32) + r1[i, h, 2].astype(F32)
            if h == 0:
                terms[i, z, :, A] = (terms[i, z, :, A].astype(F32) + v).astype(BF)
            else:
                terms[i, :, x, B] = (terms[i, :, x, B].astype(F32) + v).astype(BF)
            for k in (2, 1, 3):
                z2_copy(i, h, k).start()

    def stage_out(i):
        cols = lanes(i, R)
        arrived(r2.at[i], z2_r.at[i])
        for h, half in ((0, A), (1, B)):
            v = terms[i, z, x, half].astype(F32)
            for k in (0, 1, 2):
                v = v + r2[i, h, k].astype(F32)
            out[half, cols] = v.astype(BF)

    def step(u, _):
        t = u - LS

        @pl.when((t >= 0) & (t < S))
        def _():
            stage_own(t)
            stage_merge(t)

        @pl.when(t + LS < S)
        def _():
            stage_sib(t + LS)

        def lag(n, f):
            s = t - n

            @pl.when((s >= 0) & (s < S))
            def _():
                f(s)

        def lag_i(n, f, most):
            s = t - n

            @pl.when((s >= 0) & (s < most * NJ) & (lax.rem(s + 2 * S, NJ) == NJ - 1))
            def _():
                f(s // NJ)

        lag(LC, stage_c)
        lag(LD, stage_d)
        lag(LE, stage_e)
        lag(LF, stage_f)
        lag_i(LG, stage_g, NI - 2)
        lag_i(LZ, stage_z, NT + 1)
        lag_i(LO, stage_out, NT)
        return 0

    lax.fori_loop(0, S + LD + LS, step, 0)
    for s in range(S + LD - LF, S + LD - LE):
        stage_f(s)
    for s in range(S + LD - LE, S - 1):
        stage_e(s)
        stage_f(s)

    stage_g(NI - 2)
    stage_part()
    stage_e(S - 1)
    stage_f(S - 1)
    stage_rest()
    for i in range(NT + 1, NI):
        stage_z(i)
    for i in range(NT, NI):
        stage_out(i)

    def entry_sent():
        for ref, sem in ((r2.at[pl.ds(1, NI - 1)], t1_s), (r1.at[pl.ds(1, NI - 1)], t2_s), (r2.at[pl.ds(0, 5)], l_s), (sibs, d_s), (yr, y_s), (yr.at[:, :, :, pl.ds(0, FB)], h_s),
                         (hid.at[:, :, pl.ds(0, FF // 2)], f_s), (r1, z1_s), (r2, z2_s)):
            sent(ref, sem)

    entry_sent()


def body(tokens, gate_weight, up_weight, down_weight):
    V = pltpu.VMEM
    D = pltpu.SemaphoreType.DMA
    result = pl.pallas_call(
        kernel,
        out_shape=jax.ShapeDtypeStruct((XB, ROWS), BF),
        in_specs=[pl.BlockSpec(memory_space=pl.ANY)] * 4,
        out_specs=pl.BlockSpec(memory_space=V),
        scratch_shapes=[
            V((2 * NJ, K, 2 * FB), BF),
            V((FF, K), BF),
            V((NI, 4, 4, XB, R), BF),
            V((2, R, K), BF),
            V((S, R, 2 * FB), BF),
            V((S, R, 2 * FB), BF),
            V((S, R, 2 * FB), BF),
            V((R, 2 * FB), F32),
            V((R, K), F32),
            V((S, 3, Q, 2 * FB), BF),
            V((NI, R, FF), BF),
            V((NI, 4, 4, XB, R), BF),
            V((NI, 2, 3, 4, HB, R), BF),
            V((NI, 2, 3, HB, R), BF),
            D((2 * NJ,)), D(()), D(()),
            D(()), D((NI,)), D(()), D((NI,)),
            D(()), D((NS,)), D(()), D((NS,)), D((NS,)), D(()), D((NS,)), D((S,)), D(()), D((NI + 1,)),
            D(()), D((NI,)), D(()), D((NI,)), D(()),
        ],
        compiler_params=pltpu.CompilerParams(
            collective_id=0, has_side_effects=True, vmem_limit_bytes=60 * 2**20),
    )(tokens.T, gate_weight, up_weight, down_weight)
    return result.T


def solution(mesh):
    placed = (P(None, ("gx", "yz")), P("gx", "yz"), P("gx", "yz"), P("yz", "gx"))
    return jax.shard_map(
        body, mesh=mesh, in_specs=placed, out_specs=P(None, ("gx", "yz")), check_vma=False
    )
```
